32 devices in a mesh: groups: 2 (over x), corpus: 4 (over y, core), query: 4 (over z).
Axes of the slice: x: 2, y: 2, z: 4, core: 2. Of those that a mesh axis runs over, the one named last changes fastest.
Arguments:
- queries: bfloat16 [32, 32, 128], P(('groups', 'corpus', 'query')), parts along dimension 0, may hold values from -0.5 to 0.5
- passages: bfloat16 [4096, 180, 128], P(('groups', 'corpus', 'query')), parts along dimension 0, may hold values from -0.5 to 0.5
- token_lengths: int32 [4096], P('groups'), parts along dimension 0, may hold values from 19 to 180
- candidates: int32 [32, 256], P(('groups', 'corpus', 'query')), parts along dimension 0, may hold values from 0 to 2047, as said below
- passage_home: int32 [4096], P('groups'), parts along dimension 0, may hold values from 0 to 2047, as said below
Outputs:
- top_scores: float32 [32, 100], P(('groups', 'corpus', 'query')), parts along dimension 0
The draws below stay inside these ranges and needn't reach their ends.
There are 2 independent parts, one for each index of `groups`. The reference program is written for one: setup_inputs(seed, part) draws one part's arguments, and reference() takes and returns one part's arrays. A program takes and returns all parts, laid end to end along the dimension named above; each array names one. Nothing has to cross between parts.
Inputs may be any that keep to these rules, and one draw needn't show every extreme that they name: A permutation of the stored rows; passage id c is stored on device passage_home[c] // 128 of corpus+query. The 256 candidates of a query are distinct; among the 256 candidates of one device's queries at most 32 are stored on any one device, and exactly 32 on some device.
All inputs are finite; a program needn't handle non-finite values.
Results may differ from the reference program's by a relative error of at most 0.0003.
Values may be sent and summed in bfloat16 or wider, within the bound.
A program may use at most 128 MiB of HBM per device.

```python
import jax
import jax.numpy as jnp
from jax import lax

DIM = 128
QT = 32
PT = 180
CAND = 256
TOPK = 100
Q_DEV = 1
P_DEV = 128
SHARDS = 16
PASSAGES = 2048
QUERIES = 16
CAP = 32


def draw_passage_home(key, part):
    return jax.random.permutation(jax.random.fold_in(key, 11), PASSAGES).astype(jnp.int32)


def draw_candidates(key, part):
    home_rows = draw_passage_home(key, part)
    passage_of = jnp.argsort(home_rows, stable=True).astype(jnp.int32)
    block_keys = jax.random.split(jax.random.fold_in(key, 23), SHARDS)

    def one_block(block_key):
        hot_key, level_key, noise_key, base_key, order_key = jax.random.split(block_key, 5)
        hottest = jax.random.randint(hot_key, (), 0, SHARDS)
        levels = jax.random.randint(level_key, (SHARDS,), 0, 4)
        jitter = jax.random.randint(noise_key, (SHARDS, CAP), 0, 32768)
        shard_ids = jnp.arange(SHARDS, dtype=jnp.int32)
        boosts = jnp.where(shard_ids == hottest, 131072, 0) + levels * 16384
        slot_index = jnp.arange(SHARDS * CAP, dtype=jnp.int32).reshape(SHARDS, CAP)
        priority = (boosts[:, None] + jitter) * (SHARDS * CAP) + slot_index
        chosen = lax.top_k(priority.reshape(-1), Q_DEV * CAND)[1].astype(jnp.int32)
        shard_of = chosen // CAP
        slot_of = chosen % CAP
        offsets = jax.random.randint(base_key, (SHARDS,), 0, P_DEV)
        stored_rows = shard_of * P_DEV + (offsets[shard_of] + slot_of) % P_DEV
        shuffle = jax.random.permutation(order_key, Q_DEV * CAND)
        return passage_of[stored_rows[shuffle]].reshape(Q_DEV, CAND)
    return jax.vmap(one_block)(block_keys).reshape(QUERIES, CAND).astype(jnp.int32)


def with_ends(drawn, key, least, top_value):
    shape = drawn.shape
    spot = [jax.random.randint(jax.random.fold_in(key, axis), (), 0, shape[axis]) for axis in range(len(shape))]
    drawn = drawn.at[tuple(spot)].set(least)
    longest = shape.index(max(shape))
    spot[longest] = (spot[longest] + 1) % shape[longest]
    return drawn.at[tuple(spot)].set(top_value)


def block_levels(stream_key, extent, cuts, least, top_value):
    factor_of = 1.0
    for axis_at, parts in cuts:
        steps = jax.random.uniform(jax.random.fold_in(jax.random.fold_in(stream_key, 6), axis_at), (parts,), jnp.float32, least / len(cuts), top_value / len(cuts))
        factor_of = factor_of * jnp.repeat(jnp.exp(steps), extent[axis_at] // parts).reshape((-1,) + (1,) * (len(extent) - 1 - axis_at))
    return factor_of


def gaussian(own_key, dims, scale, reach, cuts=(), kind=jnp.bfloat16):
    drawn = jax.random.normal(own_key, dims, jnp.float32) * scale
    if len(cuts) > 0:
        drawn = block_levels(own_key, dims, cuts, -0.22, 0.18) * drawn
    return jnp.clip(drawn, min=-reach, max=reach).astype(kind)


def setup_inputs(seed: int = 0, part: int = 0) -> dict:
    key_list = jax.random.split(jax.random.key(seed), 6)
    own_keys = jax.random.split(jax.random.fold_in(key_list[5], part), 6)
    return {
        "queries": gaussian(own_keys[0], (QUERIES, QT, DIM), DIM ** -0.5, 0.5, ((0, 16),)),
        "passages": gaussian(own_keys[1], (PASSAGES, PT, DIM), DIM ** -0.5, 0.5, ((0, 16),)),
        "token_lengths": with_ends(jax.random.randint(own_keys[2], (PASSAGES,), PT // 10 + 1, PT + 1), jax.random.fold_in(own_keys[2], 1), PT // 10 + 1, PT).astype(jnp.int32),
        "candidates": draw_candidates(jax.random.fold_in(jax.random.fold_in(key_list[5], part), 71), part),
        "passage_home": draw_passage_home(jax.random.fold_in(jax.random.fold_in(key_list[5], part), 71), part),
    }


def pair_scores(query_tok, blocks, pair_lengths):
    similar = jnp.einsum("qd,npd->nqp", query_tok.astype(jnp.float32), blocks.astype(jnp.float32), precision=lax.Precision.HIGHEST)
    inside = jnp.arange(blocks.shape[1], dtype=jnp.int32)[None, None, :] < pair_lengths[:, None, None]
    return jnp.sum(jnp.max(jnp.where(inside, similar, -1e30), axis=2), axis=1)


def reference(queries, passages, token_lengths, candidates, passage_home):
    def one_query(paired):
        query_tok, cand_ids = paired
        stored = passage_home[cand_ids]
        scores = pair_scores(query_tok, passages[stored], token_lengths[cand_ids])
        return lax.top_k(scores, TOPK)[0]
    return lax.map(one_query, (queries, candidates))
```

```python
import functools

import jax
import jax.numpy as jnp
from jax import lax
from jax.experimental import pallas as pl
from jax.experimental.pallas import tpu as pltpu
from jax.sharding import PartitionSpec as P

TOPK = 100
LANES = 128
MESH = pl.DeviceIdType.MESH
F32, BF16, I32 = jnp.float32, jnp.bfloat16, jnp.int32


def split3(x):
    hi = x.astype(BF16)
    rest = x - hi.astype(F32)
    mid = rest.astype(BF16)
    return hi, mid, (rest - mid.astype(F32)).astype(BF16)


def dot_nt(a, b):
    return lax.dot_general(a, b, (((1,), (1,)), ((), ())), preferred_element_type=F32)


def kernel(
    shards, inner, tile, chunk, band,
    q_ref, pass_ref, len_ref, cand_ref, home_ref, out_ref,
    slab, qbuf, lens, best, sent, got, where_row,
    load_sem, qs_sem, qr_sem, ss_sem, sr_sem,
):
    slots, slab_rows, width = slab.shape
    tokens = qbuf.shape[1]
    me = lax.axis_index("corpus") * inner + lax.axis_index("query")
    chunks = slots // chunk

    def load(c):
        part = pl.ds(c * chunk, chunk)
        return pltpu.make_async_copy(pass_ref.at[part], slab.at[part], load_sem.at[c])

    for c in range(chunks):
        load(c).start()

    def peer(d):
        p = lax.rem(me + d, shards)
        return p, {"corpus": p // inner, "query": lax.rem(p, inner)}

    barrier = pltpu.get_barrier_semaphore()

    def greet(d, carry):
        pl.semaphore_signal(barrier, inc=1, device_id=peer(d)[1], device_id_type=MESH)
        return carry

    lax.fori_loop(1, shards, greet, 0)
    pl.semaphore_wait(barrier, shards - 1)

    def query_copy(slot, sem_s, device):
        return pltpu.make_async_remote_copy(
            src_ref=q_ref, dst_ref=qbuf.at[pl.ds(slot, 1)],
            send_sem=qs_sem.at[sem_s], recv_sem=qr_sem.at[slot],
            device_id=device, device_id_type=MESH,
        )

    def score_copy(row, slot, device):
        return pltpu.make_async_remote_copy(
            src_ref=sent.at[row], dst_ref=got.at[slot],
            send_sem=ss_sem.at[row], recv_sem=sr_sem.at[slot],
            device_id=device, device_id_type=MESH,
        )

    def send_query(d, carry):
        p, device = peer(d)
        query_copy(me, p, device).start()
        return carry

    lax.fori_loop(1, shards, send_query, 0)
    qbuf[pl.ds(me, 1)] = q_ref[...]

    stored = lax.broadcasted_iota(I32, (slab_rows, LANES), 0) + me * slab_rows
    picked = jnp.zeros((slab_rows, LANES), I32)
    for b in range(home_ref.shape[0]):
        hit = home_ref[b : b + 1, :] == stored
        picked = jnp.where(hit, len_ref[b : b + 1, :], picked)
    ones = jnp.ones((LANES, LANES), BF16)
    lens[...] = jnp.dot(
        picked.astype(F32).astype(BF16), ones, preferred_element_type=F32
    ).astype(I32)

    count = cand_ref.shape[1]
    cand = cand_ref[...]
    low = lax.broadcasted_iota(I32, (LANES, count), 0) == lax.rem(cand, LANES)
    low = jnp.where(low, 1.0, 0.0).astype(BF16)
    home = home_ref[...]
    blocks = home.shape[0]
    high = lax.broadcasted_iota(I32, (blocks, count), 0) == cand // LANES
    for k, part in enumerate((home // slab_rows, lax.rem(home, slab_rows))):
        table = jnp.dot(part.astype(F32).astype(BF16), low, preferred_element_type=F32)
        where_row[k : k + 1, :] = jnp.sum(
            jnp.where(high, table, 0.0), axis=0, keepdims=True
        ).astype(I32)

    def wait_load(c, carry):
        load(c).wait()
        return carry

    lax.fori_loop(0, chunks, wait_load, 0)

    columns = tile * tokens
    tiles = shards // tile
    group = lax.broadcasted_iota(I32, (tile, columns), 0)
    member = lax.broadcasted_iota(I32, (tile, columns), 1) // tokens
    adder = jnp.where(group == member, 1.0, 0.0).astype(BF16)

    def one_tile(b, carry):
        t = lax.rem(me // tile + b, tiles)

        def wait_query(i, c):
            p = t * tile + i

            @pl.when(p != me)
            def _():
                query_copy(p, p, {"query": lax.axis_index("query")}).wait_recv()

            return c

        lax.fori_loop(0, tile, wait_query, 0)
        query = qbuf[pl.ds(t * tile, tile)].reshape(columns, width)

        for r in range(0, slab_rows, band):
            live = lens[r : r + band, :]

            def some_slots(g, top):
                block = slab[pl.ds(g * chunk, chunk), r : r + band, :]
                similar = dot_nt(block.reshape(chunk * band, width), query)
                for u in range(chunk):
                    inside = live > g * chunk + u
                    row = similar[u * band : (u + 1) * band]
                    top = tuple(
                        jnp.maximum(
                            old,
                            jnp.where(inside, row[:, k * LANES : (k + 1) * LANES], -1e30),
                        )
                        for k, old in enumerate(top)
                    )
                return top

            start = tuple(
                jnp.full((band, LANES), -1e30, F32) for _ in range(columns // LANES)
            )
            top = lax.fori_loop(0, chunks, some_slots, start)
            best[r : r + band, :] = jnp.concatenate(top, axis=1)
        hi, mid, lo = split3(best[...])
        scores = dot_nt(adder, lo) + dot_nt(adder, mid) + dot_nt(adder, hi)
        for i in range(tile):
            p = t * tile + i
            sent[pl.ds(p, 1)] = scores[i : i + 1].reshape(1, 1, slab_rows)

            @pl.when(p != me)
            def _():
                device = {"corpus": p // inner, "query": lax.rem(p, inner)}
                score_copy(p, me, device).start()

            @pl.when(p == me)
            def _():
                got[pl.ds(p, 1)] = scores[i : i + 1].reshape(1, 1, slab_rows)

        return carry

    lax.fori_loop(0, tiles, one_tile, 0)

    def wait_scores(d, carry):
        p, device = peer(d)
        score_copy(p, p, device).wait_recv()
        return carry

    lax.fori_loop(1, shards, wait_scores, 0)
    table = got[...].reshape(shards, slab_rows)
    offset = lax.broadcasted_iota(I32, (slab_rows, count), 0) == where_row[1:2, :]
    offset = jnp.where(offset, 1.0, 0.0).astype(BF16)
    hi, mid, lo = split3(table)
    dot = functools.partial(jnp.dot, preferred_element_type=F32)
    found = (dot(hi, offset) + dot(mid, offset)) + dot(lo, offset)
    shard = lax.broadcasted_iota(I32, (shards, count), 0) == where_row[0:1, :]
    score = jnp.sum(jnp.where(shard, found, 0.0), axis=0, keepdims=True)

    down = jnp.transpose(jnp.broadcast_to(score, (LANES, count)))
    mine = lax.broadcasted_iota(I32, (count, LANES), 0)
    rank = jnp.zeros((count, LANES), F32)
    for k in range(0, count, LANES):
        other = lax.broadcasted_iota(I32, (count, LANES), 1) + k
        across = score[:, k : k + LANES]
        ahead = (across > down) | ((across == down) & (other < mine))
        rank += jnp.where(ahead, 1.0, 0.0)
    rank = jnp.dot(rank.astype(BF16), ones, preferred_element_type=F32)
    slot = lax.broadcasted_iota(I32, (count, LANES), 1).astype(F32)
    ranked = jnp.sum(jnp.where(rank == slot, down, 0.0), axis=0, keepdims=True)
    out_ref[...] = ranked[:, : out_ref.shape[1]]

    def wait_sends(d, carry):
        p, device = peer(d)
        query_copy(p, p, device).wait_send()
        score_copy(p, p, device).wait_send()
        return carry

    lax.fori_loop(1, shards, wait_sends, 0)


def on_device(queries, passages, token_lengths, candidates, passage_home):
    inner = lax.axis_size("query")
    shards = lax.axis_size("corpus") * inner
    slab_rows, slots, width = passages.shape
    tokens = queries.shape[1]
    count = candidates.shape[1]
    tile = max(1, 256 // tokens)
    while shards % tile:
        tile -= 1
    chunk = next(c for c in range(12, 0, -1) if slots % c == 0)
    band = 32
    by_slot = jnp.transpose(passages, (1, 0, 2))
    vmem = pl.BlockSpec(memory_space=pltpu.VMEM)
    return pl.pallas_call(
        functools.partial(kernel, shards, inner, tile, chunk, band),
        out_shape=jax.ShapeDtypeStruct((1, TOPK), F32),
        in_specs=[vmem, pl.BlockSpec(memory_space=pltpu.HBM), vmem, vmem, vmem],
        out_specs=vmem,
        scratch_shapes=[
            pltpu.VMEM(by_slot.shape, BF16),
            pltpu.VMEM((shards, tokens, width), BF16),
            pltpu.VMEM((slab_rows, LANES), I32),
            pltpu.VMEM((slab_rows, tile * tokens), F32),
            pltpu.VMEM((shards, 1, slab_rows), F32),
            pltpu.VMEM((shards, 1, slab_rows), F32),
            pltpu.VMEM((8, count), I32),
            pltpu.SemaphoreType.DMA((slots // chunk,)),
            pltpu.SemaphoreType.DMA((shards,)),
            pltpu.SemaphoreType.DMA((shards,)),
            pltpu.SemaphoreType.DMA((shards,)),
            pltpu.SemaphoreType.DMA((shards,)),
        ],
        compiler_params=pltpu.CompilerParams(
            collective_id=0, has_side_effects=True, vmem_limit_bytes=32 * 1024 * 1024
        ),
    )(
        queries,
        by_slot,
        token_lengths.reshape(-1, LANES),
        candidates,
        passage_home.reshape(-1, LANES),
    )


def solution(mesh):
    placed = (
        P(("groups", "corpus", "query"), None, None),
        P(("groups", "corpus", "query"), None, None),
        P("groups"),
        P(("groups", "corpus", "query"), None),
        P("groups"),
    )
    return jax.shard_map(
        on_device,
        mesh=mesh,
        in_specs=placed,
        out_specs=P(("groups", "corpus", "query"), None),
        check_vma=False,
    )
```

```python
import functools

import jax
import jax.numpy as jnp
from jax import lax
from jax.experimental import pallas as pl
from jax.experimental.pallas import tpu as pltpu
from jax.sharding import PartitionSpec as P

TOPK = 100
LANES = 128
CHUNK, BAND, COLUMNS = 20, 128, 256
MESH = pl.DeviceIdType.MESH
F32, BF16, I32 = jnp.float32, jnp.bfloat16, jnp.int32


def split3(x):
    hi = x.astype(BF16)
    rest = x - hi.astype(F32)
    mid = rest.astype(BF16)
    return hi, mid, (rest - mid.astype(F32)).astype(BF16)


def dot_nt(a, b):
    return lax.dot_general(a, b, (((1,), (1,)), ((), ())), preferred_element_type=F32)


def kernel(
    shards, inner, tile, chunk, band,
    q_ref, pass_ref, len_hbm, cand_hbm, home_hbm, out_ref,
    len_ref, cand_ref, home_ref, slab, query_t, qbuf, lens, best, sent, got, where_row,
    small_sem, load_sem, qs_sem, qr_sem, ss_sem, sr_sem,
):
    slots, slab_rows, width = slab.shape
    tokens = qbuf.shape[1]
    me = lax.axis_index("corpus") * inner + lax.axis_index("query")
    chunks = slots // chunk

    def load(c):
        part = pl.ds(c * chunk, chunk)
        return pltpu.make_async_copy(pass_ref.at[part], slab.at[part], load_sem.at[c])

    def peer(d):
        p = lax.rem(me + d, shards)
        return p, {"corpus": p // inner, "query": lax.rem(p, inner)}

    barrier = pltpu.get_barrier_semaphore()

    def greet(d, carry):
        pl.semaphore_signal(barrier, inc=1, device_id=peer(d)[1], device_id_type=MESH)
        return carry

    lax.fori_loop(1, shards, greet, 0)
    small = [
        pltpu.make_async_copy(src, dst, small_sem.at[k])
        for k, (src, dst) in enumerate(
            (
                (home_hbm, home_ref),
                (len_hbm, len_ref),
                (cand_hbm, cand_ref),
                (q_ref, qbuf.at[pl.ds(me, 1)]),
            )
        )
    ]
    for copy in small:
        copy.start()
    for c in range(chunks):
        load(c).start()
    pl.semaphore_wait(barrier, shards - 1)

    def query_copy(slot, sem_s, device):
        return pltpu.make_async_remote_copy(
            src_ref=q_ref, dst_ref=qbuf.at[pl.ds(slot, 1)],
            send_sem=qs_sem.at[sem_s], recv_sem=qr_sem.at[slot],
            device_id=device, device_id_type=MESH,
        )

    def score_copy(row, slot, device):
        return pltpu.make_async_remote_copy(
            src_ref=sent.at[row], dst_ref=got.at[slot],
            send_sem=ss_sem.at[row], recv_sem=sr_sem.at[slot],
            device_id=device, device_id_type=MESH,
        )

    def send_query(d, carry):
        p, device = peer(d)
        query_copy(me, p, device).start()
        return carry

    lax.fori_loop(1, shards, send_query, 0)
    for copy in small:
        copy.wait()

    stored = lax.broadcasted_iota(I32, (slab_rows, LANES), 0) + me * slab_rows
    picked = jnp.zeros((slab_rows, LANES), I32)
    for b in range(home_ref.shape[0]):
        hit = home_ref[b : b + 1, :] == stored
        picked = jnp.where(hit, len_ref[b : b + 1, :], picked)
    ones = jnp.ones((LANES, LANES), BF16)
    lens[...] = jnp.dot(
        picked.astype(F32).astype(BF16), ones, preferred_element_type=F32
    ).astype(I32)

    count = cand_ref.shape[1]
    cand = cand_ref[...]
    low = lax.broadcasted_iota(I32, (LANES, count), 0) == lax.rem(cand, LANES)
    low = jnp.where(low, 1.0, 0.0).astype(BF16)
    home = home_ref[...]
    blocks = home.shape[0]
    high = lax.broadcasted_iota(I32, (blocks, count), 0) == cand // LANES
    for k, part in enumerate((home // slab_rows, lax.rem(home, slab_rows))):
        table = jnp.dot(part.astype(F32).astype(BF16), low, preferred_element_type=F32)
        where_row[k : k + 1, :] = jnp.sum(
            jnp.where(high, table, 0.0), axis=0, keepdims=True
        ).astype(I32)

    def wait_load(c, carry):
        load(c).wait()
        return carry

    lax.fori_loop(0, chunks, wait_load, 0)

    columns = tile * tokens
    tiles = shards // tile
    group = lax.broadcasted_iota(I32, (tile, columns), 0)
    member = lax.broadcasted_iota(I32, (tile, columns), 1) // tokens
    adder = jnp.where(group == member, 1.0, 0.0).astype(BF16)

    def one_tile(b, carry):
        t = lax.rem(me // tile + b, tiles)

        def wait_query(i, c):
            p = t * tile + i

            @pl.when(p != me)
            def _():
                query_copy(p, p, {"query": lax.axis_index("query")}).wait_recv()

            return c

        lax.fori_loop(0, tile, wait_query, 0)
        query_t[...] = qbuf[pl.ds(t * tile, tile)].reshape(columns, width).T

        for r in range(0, slab_rows, band):
            live = lens[r : r + band, :]

            def some_slots(g, top):
                block = slab[pl.ds(g * chunk, chunk), r : r + band, :]
                similar = jnp.dot(
                    block.reshape(chunk * band, width), query_t[...],
                    preferred_element_type=F32,
                )
                for u in range(chunk):
                    inside = live > g * chunk + u
                    row = similar[u * band : (u + 1) * band]
                    top = tuple(
                        jnp.maximum(
                            old,
                            jnp.where(inside, row[:, k * LANES : (k + 1) * LANES], -1e30),
                        )
                        for k, old in enumerate(top)
                    )
                return top

            start = tuple(
                jnp.full((band, LANES), -1e30, F32) for _ in range(columns // LANES)
            )
            top = lax.fori_loop(0, chunks, some_slots, start)
            best[r : r + band, :] = jnp.concatenate(top, axis=1)
        hi, mid, lo = split3(best[...])
        scores = dot_nt(adder, lo) + dot_nt(adder, mid) + dot_nt(adder, hi)
        for i in range(tile):
            p = t * tile + i
            sent[pl.ds(p, 1)] = scores[i : i + 1].reshape(1, 1, slab_rows)

            @pl.when(p != me)
            def _():
                device = {"corpus": p // inner, "query": lax.rem(p, inner)}
                score_copy(p, me, device).start()

            @pl.when(p == me)
            def _():
                got[pl.ds(p, 1)] = scores[i : i + 1].reshape(1, 1, slab_rows)

        return carry

    lax.fori_loop(0, tiles, one_tile, 0)

    def wait_scores(d, carry):
        p, device = peer(d)
        score_copy(p, p, device).wait_recv()
        return carry

    lax.fori_loop(1, shards, wait_scores, 0)
    table = got[...].reshape(shards, slab_rows)
    offset = lax.broadcasted_iota(I32, (slab_rows, count), 0) == where_row[1:2, :]
    offset = jnp.where(offset, 1.0, 0.0).astype(BF16)
    hi, mid, lo = split3(table)
    dot = functools.partial(jnp.dot, preferred_element_type=F32)
    found = (dot(hi, offset) + dot(mid, offset)) + dot(lo, offset)
    shard = lax.broadcasted_iota(I32, (shards, count), 0) == where_row[0:1, :]
    score = jnp.sum(jnp.where(shard, found, 0.0), axis=0, keepdims=True)

    down = jnp.transpose(jnp.broadcast_to(score, (LANES, count)))
    mine = lax.broadcasted_iota(I32, (count, LANES), 0)
    rank = jnp.zeros((count, LANES), F32)
    for k in range(0, count, LANES):
        other = lax.broadcasted_iota(I32, (count, LANES), 1) + k
        across = score[:, k : k + LANES]
        ahead = (across > down) | ((across == down) & (other < mine))
        rank += jnp.where(ahead, 1.0, 0.0)
    rank = jnp.dot(rank.astype(BF16), ones, preferred_element_type=F32)
    slot = lax.broadcasted_iota(I32, (count, LANES), 1).astype(F32)
    ranked = jnp.sum(jnp.where(rank == slot, down, 0.0), axis=0, keepdims=True)
    out_ref[...] = ranked[:, : out_ref.shape[1]]

    def wait_sends(d, carry):
        p, device = peer(d)
        query_copy(p, p, device).wait_send()
        score_copy(p, p, device).wait_send()
        return carry

    lax.fori_loop(1, shards, wait_sends, 0)


def on_device(queries, passages, token_lengths, candidates, passage_home):
    inner = lax.axis_size("query")
    shards = lax.axis_size("corpus") * inner
    slab_rows, slots, width = passages.shape
    tokens = queries.shape[1]
    count = candidates.shape[1]
    tile = max(1, COLUMNS // tokens)
    while shards % tile:
        tile -= 1
    chunk = next(c for c in range(CHUNK, 0, -1) if slots % c == 0)
    band = BAND if slab_rows % BAND == 0 else slab_rows
    by_slot = jnp.transpose(passages, (1, 0, 2))
    vmem = pl.BlockSpec(memory_space=pltpu.VMEM)
    return pl.pallas_call(
        functools.partial(kernel, shards, inner, tile, chunk, band),
        out_shape=jax.ShapeDtypeStruct((1, TOPK), F32),
        in_specs=[pl.BlockSpec(memory_space=pltpu.HBM)] * 5,
        out_specs=vmem,
        scratch_shapes=[
            pltpu.VMEM((len(token_lengths) // LANES, LANES), I32),
            pltpu.VMEM(candidates.shape, I32),
            pltpu.VMEM((len(passage_home) // LANES, LANES), I32),
            pltpu.VMEM(by_slot.shape, BF16),
            pltpu.VMEM((width, tile * tokens), BF16),
            pltpu.VMEM((shards, tokens, width), BF16),
            pltpu.VMEM((slab_rows, LANES), I32),
            pltpu.VMEM((slab_rows, tile * tokens), F32),
            pltpu.VMEM((shards, 1, slab_rows), F32),
            pltpu.VMEM((shards, 1, slab_rows), F32),
            pltpu.VMEM((8, count), I32),
            pltpu.SemaphoreType.DMA((4,)),
            pltpu.SemaphoreType.DMA((slots // chunk,)),
            pltpu.SemaphoreType.DMA((shards,)),
            pltpu.SemaphoreType.DMA((shards,)),
            pltpu.SemaphoreType.DMA((shards,)),
            pltpu.SemaphoreType.DMA((shards,)),
        ],
        compiler_params=pltpu.CompilerParams(
            collective_id=0, has_side_effects=True, vmem_limit_bytes=56 * 1024 * 1024
        ),
    )(
        queries,
        by_slot,
        token_lengths.reshape(-1, LANES),
        candidates,
        passage_home.reshape(-1, LANES),
    )


def solution(mesh):
    placed = (
        P(("groups", "corpus", "query"), None, None),
        P(("groups", "corpus", "query"), None, None),
        P("groups"),
        P(("groups", "corpus", "query"), None),
        P("groups"),
    )
    return jax.shard_map(
        on_device,
        mesh=mesh,
        in_specs=placed,
        out_specs=P(("groups", "corpus", "query"), None),
        check_vma=False,
    )
```

```python
import functools

import jax
import jax.numpy as jnp
from jax import lax
from jax.experimental import pallas as pl
from jax.experimental.pallas import tpu as pltpu
from jax.sharding import PartitionSpec as P

TOPK = 100
LANES = 128
CHUNK, BAND, COLUMNS = 20, 128, 256
MESH = pl.DeviceIdType.MESH
F32, BF16, I32 = jnp.float32, jnp.bfloat16, jnp.int32


def split3(x):
    hi = x.astype(BF16)
    rest = x - hi.astype(F32)
    mid = rest.astype(BF16)
    return hi, mid, (rest - mid.astype(F32)).astype(BF16)


def dot_nt(a, b):
    return lax.dot_general(a, b, (((1,), (1,)), ((), ())), preferred_element_type=F32)


def kernel(
    shards, inner, tile, chunk, band,
    q_ref, pass_ref, len_hbm, cand_hbm, home_hbm, out_ref,
    len_ref, cand_ref, home_ref, slab, query_t, qbuf, lens, best, sent, got, where_row,
    small_sem, load_sem, qs_sem, qr_sem, ps_sem, pr_sem, ss_sem, sr_sem,
):
    slots, slab_rows, width = slab.shape
    tokens = qbuf.shape[1]
    mesh_me = lax.axis_index("corpus") * inner + lax.axis_index("query")
    half = shards // 2
    plane = lax.rem(lax.axis_index("corpus"), 2)
    spot = (lax.axis_index("corpus") // 2) * inner + lax.axis_index("query")
    me = plane * half + spot

    def device_of(p):
        rest = lax.rem(p, half)
        corpus = (rest // inner) * 2 + p // half
        query = lax.rem(rest, inner)
        return corpus * inner + query, {"corpus": corpus, "query": query}

    chunks = slots // chunk

    def load(c):
        part = pl.ds(c * chunk, chunk)
        return pltpu.make_async_copy(pass_ref.at[part], slab.at[part], load_sem.at[c])

    def peer(d):
        p = lax.rem(me + d, shards)
        return p, *device_of(p)

    barrier = pltpu.get_barrier_semaphore()

    def greet(d, carry):
        pl.semaphore_signal(barrier, inc=1, device_id=peer(d)[2], device_id_type=MESH)
        return carry

    lax.fori_loop(1, shards, greet, 0)
    small = [
        pltpu.make_async_copy(src, dst, small_sem.at[k])
        for k, (src, dst) in enumerate(
            (
                (home_hbm, home_ref),
                (len_hbm, len_ref),
                (cand_hbm, cand_ref),
                (q_ref, qbuf.at[pl.ds(me, 1)]),
            )
        )
    ]
    for copy in small:
        copy.start()
    for c in range(chunks):
        load(c).start()
    pl.semaphore_wait(barrier, shards - 1)

    def query_copy(slot, sem_s, device):
        return pltpu.make_async_remote_copy(
            src_ref=q_ref, dst_ref=qbuf.at[pl.ds(slot, 1)],
            send_sem=qs_sem.at[sem_s], recv_sem=qr_sem.at[slot],
            device_id=device, device_id_type=MESH,
        )

    def score_copy(row, slot, device):
        return pltpu.make_async_remote_copy(
            src_ref=sent.at[row], dst_ref=got.at[slot],
            send_sem=ss_sem.at[row], recv_sem=sr_sem.at[slot],
            device_id=device, device_id_type=MESH,
        )

    def plane_copy(which):
        part = pl.ds(which * half, half)
        return pltpu.make_async_remote_copy(
            src_ref=qbuf.at[part], dst_ref=qbuf.at[part],
            send_sem=ps_sem, recv_sem=pr_sem,
            device_id=device_of((1 - plane) * half + spot)[1], device_id_type=MESH,
        )

    def send_query(d, carry):
        p = plane * half + lax.rem(spot + d, half)
        query_copy(me, p, device_of(p)[1]).start()
        return carry

    lax.fori_loop(1, half, send_query, 0)
    for copy in small:
        copy.wait()

    stored = lax.broadcasted_iota(I32, (slab_rows, LANES), 0) + mesh_me * slab_rows
    picked = jnp.zeros((slab_rows, LANES), I32)
    for b in range(home_ref.shape[0]):
        hit = home_ref[b : b + 1, :] == stored
        picked = jnp.where(hit, len_ref[b : b + 1, :], picked)
    ones = jnp.ones((LANES, LANES), BF16)
    lens[...] = jnp.dot(
        picked.astype(F32).astype(BF16), ones, preferred_element_type=F32
    ).astype(I32)

    count = cand_ref.shape[1]
    cand = cand_ref[...]
    low = lax.broadcasted_iota(I32, (LANES, count), 0) == lax.rem(cand, LANES)
    low = jnp.where(low, 1.0, 0.0).astype(BF16)
    home = home_ref[...]
    blocks = home.shape[0]
    high = lax.broadcasted_iota(I32, (blocks, count), 0) == cand // LANES
    for k, part in enumerate((home // slab_rows, lax.rem(home, slab_rows))):
        table = jnp.dot(part.astype(F32).astype(BF16), low, preferred_element_type=F32)
        where_row[k : k + 1, :] = jnp.sum(
            jnp.where(high, table, 0.0), axis=0, keepdims=True
        ).astype(I32)

    def wait_query(d, carry):
        p = plane * half + lax.rem(spot + d, half)
        query_copy(p, p, device_of(p)[1]).wait_recv()
        return carry

    lax.fori_loop(1, half, wait_query, 0)
    plane_copy(plane).start()

    def wait_load(c, carry):
        load(c).wait()
        return carry

    lax.fori_loop(0, chunks, wait_load, 0)

    columns = tile * tokens
    tiles = half // tile
    group = lax.broadcasted_iota(I32, (tile, columns), 0)
    member = lax.broadcasted_iota(I32, (tile, columns), 1) // tokens
    adder = jnp.where(group == member, 1.0, 0.0).astype(BF16)

    def one_tile(b, carry):
        @pl.when(b == tiles)
        def _():
            plane_copy(1 - plane).wait_recv()

        t = lax.rem(plane * tiles + b, 2 * tiles)
        query_t[...] = qbuf[pl.ds(t * tile, tile)].reshape(columns, width).T

        for r in range(0, slab_rows, band):
            live = lens[r : r + band, :]

            def some_slots(g, top):
                block = slab[pl.ds(g * chunk, chunk), r : r + band, :]
                similar = jnp.dot(
                    block.reshape(chunk * band, width), query_t[...],
                    preferred_element_type=F32,
                )
                for u in range(chunk):
                    inside = live > g * chunk + u
                    row = similar[u * band : (u + 1) * band]
                    top = tuple(
                        jnp.maximum(
                            old,
                            jnp.where(inside, row[:, k * LANES : (k + 1) * LANES], -1e30),
                        )
                        for k, old in enumerate(top)
                    )
                return top

            start = tuple(
                jnp.full((band, LANES), -1e30, F32) for _ in range(columns // LANES)
            )
            top = lax.fori_loop(0, chunks, some_slots, start)
            best[r : r + band, :] = jnp.concatenate(top, axis=1)
        hi, mid, lo = split3(best[...])
        scores = dot_nt(adder, lo) + dot_nt(adder, mid) + dot_nt(adder, hi)
        for i in range(tile):
            p = t * tile + i
            sent[pl.ds(p, 1)] = scores[i : i + 1].reshape(1, 1, slab_rows)

            @pl.when(p != me)
            def _():
                score_copy(p, mesh_me, device_of(p)[1]).start()

            @pl.when(p == me)
            def _():
                got[pl.ds(mesh_me, 1)] = scores[i : i + 1].reshape(1, 1, slab_rows)

        return carry

    lax.fori_loop(0, 2 * tiles, one_tile, 0)

    def wait_scores(d, carry):
        p, slot, device = peer(d)
        score_copy(p, slot, device).wait_recv()
        return carry

    lax.fori_loop(1, shards, wait_scores, 0)
    table = got[...].reshape(shards, slab_rows)
    offset = lax.broadcasted_iota(I32, (slab_rows, count), 0) == where_row[1:2, :]
    offset = jnp.where(offset, 1.0, 0.0).astype(BF16)
    hi, mid, lo = split3(table)
    dot = functools.partial(jnp.dot, preferred_element_type=F32)
    found = (dot(hi, offset) + dot(mid, offset)) + dot(lo, offset)
    shard = lax.broadcasted_iota(I32, (shards, count), 0) == where_row[0:1, :]
    score = jnp.sum(jnp.where(shard, found, 0.0), axis=0, keepdims=True)

    down = jnp.transpose(jnp.broadcast_to(score, (LANES, count)))
    mine = lax.broadcasted_iota(I32, (count, LANES), 0)
    rank = jnp.zeros((count, LANES), F32)
    for k in range(0, count, LANES):
        other = lax.broadcasted_iota(I32, (count, LANES), 1) + k
        across = score[:, k : k + LANES]
        ahead = (across > down) | ((across == down) & (other < mine))
        rank += jnp.where(ahead, 1.0, 0.0)
    rank = jnp.dot(rank.astype(BF16), ones, preferred_element_type=F32)
    slot = lax.broadcasted_iota(I32, (count, LANES), 1).astype(F32)
    ranked = jnp.sum(jnp.where(rank == slot, down, 0.0), axis=0, keepdims=True)
    out_ref[...] = ranked[:, : out_ref.shape[1]]

    def wait_sends(d, carry):
        p, slot, device = peer(d)
        score_copy(p, slot, device).wait_send()
        return carry

    lax.fori_loop(1, shards, wait_sends, 0)

    def wait_queries(d, carry):
        p = plane * half + lax.rem(spot + d, half)
        query_copy(p, p, device_of(p)[1]).wait_send()
        return carry

    lax.fori_loop(1, half, wait_queries, 0)
    plane_copy(plane).wait_send()


def on_device(queries, passages, token_lengths, candidates, passage_home):
    inner = lax.axis_size("query")
    shards = lax.axis_size("corpus") * inner
    slab_rows, slots, width = passages.shape
    tokens = queries.shape[1]
    count = candidates.shape[1]
    tile = max(1, COLUMNS // tokens)
    while (shards // 2) % tile:
        tile -= 1
    chunk = next(c for c in range(CHUNK, 0, -1) if slots % c == 0)
    band = BAND if slab_rows % BAND == 0 else slab_rows
    by_slot = jnp.transpose(passages, (1, 0, 2))
    vmem = pl.BlockSpec(memory_space=pltpu.VMEM)
    return pl.pallas_call(
        functools.partial(kernel, shards, inner, tile, chunk, band),
        out_shape=jax.ShapeDtypeStruct((1, TOPK), F32),
        in_specs=[pl.BlockSpec(memory_space=pltpu.HBM)] * 5,
        out_specs=vmem,
        scratch_shapes=[
            pltpu.VMEM((len(token_lengths) // LANES, LANES), I32),
            pltpu.VMEM(candidates.shape, I32),
            pltpu.VMEM((len(passage_home) // LANES, LANES), I32),
            pltpu.VMEM(by_slot.shape, BF16),
            pltpu.VMEM((width, tile * tokens), BF16),
            pltpu.VMEM((shards, tokens, width), BF16),
            pltpu.VMEM((slab_rows, LANES), I32),
            pltpu.VMEM((slab_rows, tile * tokens), F32),
            pltpu.VMEM((shards, 1, slab_rows), F32),
            pltpu.VMEM((shards, 1, slab_rows), F32),
            pltpu.VMEM((8, count), I32),
            pltpu.SemaphoreType.DMA((4,)),
            pltpu.SemaphoreType.DMA((slots // chunk,)),
            pltpu.SemaphoreType.DMA((shards,)),
            pltpu.SemaphoreType.DMA((shards,)),
            pltpu.SemaphoreType.DMA,
            pltpu.SemaphoreType.DMA,
            pltpu.SemaphoreType.DMA((shards,)),
            pltpu.SemaphoreType.DMA((shards,)),
        ],
        compiler_params=pltpu.CompilerParams(
            collective_id=0, has_side_effects=True, vmem_limit_bytes=56 * 1024 * 1024
        ),
    )(
        queries,
        by_slot,
        token_lengths.reshape(-1, LANES),
        candidates,
        passage_home.reshape(-1, LANES),
    )


def solution(mesh):
    placed = (
        P(("groups", "corpus", "query"), None, None),
        P(("groups", "corpus", "query"), None, None),
        P("groups"),
        P(("groups", "corpus", "query"), None),
        P("groups"),
    )
    return jax.shard_map(
        on_device,
        mesh=mesh,
        in_specs=placed,
        out_specs=P(("groups", "corpus", "query"), None),
        check_vma=False,
    )
```

```python
import functools

import jax
import jax.numpy as jnp
from jax import lax
from jax.experimental import pallas as pl
from jax.experimental.pallas import tpu as pltpu
from jax.sharding import PartitionSpec as P

TOPK = 100
LANES = 128
CHUNK, BAND, COLUMNS = 20, 128, 256
MESH = pl.DeviceIdType.MESH
F32, BF16, I32 = jnp.float32, jnp.bfloat16, jnp.int32


def split3(x):
    hi = x.astype(BF16)
    rest = x - hi.astype(F32)
    mid = rest.astype(BF16)
    return hi, mid, (rest - mid.astype(F32)).astype(BF16)


def dot_nt(a, b):
    return lax.dot_general(a, b, (((1,), (1,)), ((), ())), preferred_element_type=F32)


def kernel(
    shards, inner, tile, chunk, band,
    q_ref, pass_ref, len_hbm, cand_hbm, home_hbm, out_ref,
    len_ref, cand_ref, home_ref, slab, query_t, qbuf, lens, best, sent, got, where_row,
    small_sem, load_sem, qs_sem, qr_sem, ps_sem, pr_sem, ss_sem, sr_sem,
):
    slots, slab_rows, width = slab.shape
    tokens = qbuf.shape[1]
    mesh_me = lax.axis_index("corpus") * inner + lax.axis_index("query")
    half = shards // 2
    plane = lax.rem(lax.axis_index("corpus"), 2)
    spot = (lax.axis_index("corpus") // 2) * inner + lax.axis_index("query")
    me = plane * half + spot

    def device_of(p):
        rest = lax.rem(p, half)
        corpus = (rest // inner) * 2 + p // half
        query = lax.rem(rest, inner)
        return corpus * inner + query, {"corpus": corpus, "query": query}

    chunks = slots // chunk

    def load(c):
        part = pl.ds(c * chunk, chunk)
        return pltpu.make_async_copy(pass_ref.at[part], slab.at[part], load_sem.at[c])

    def peer(d):
        p = lax.rem(me + d, shards)
        return p, *device_of(p)

    barrier = pltpu.get_barrier_semaphore()

    def greet(d, carry):
        pl.semaphore_signal(barrier, inc=1, device_id=peer(d)[2], device_id_type=MESH)
        return carry

    lax.fori_loop(1, shards, greet, 0)
    small = [
        pltpu.make_async_copy(src, dst, small_sem.at[k])
        for k, (src, dst) in enumerate(
            (
                (home_hbm, home_ref),
                (len_hbm, len_ref),
                (cand_hbm, cand_ref),
                (q_ref, qbuf.at[pl.ds(me, 1)]),
            )
        )
    ]
    for copy in small:
        copy.start()
    for c in range(chunks):
        load(c).start()
    pl.semaphore_wait(barrier, shards - 1)

    def query_copy(slot, sem_s, device):
        return pltpu.make_async_remote_copy(
            src_ref=qbuf.at[pl.ds(me, 1)], dst_ref=qbuf.at[pl.ds(slot, 1)],
            send_sem=qs_sem.at[sem_s], recv_sem=qr_sem.at[slot],
            device_id=device, device_id_type=MESH,
        )

    def score_copy(row, slot, device):
        return pltpu.make_async_remote_copy(
            src_ref=sent.at[row], dst_ref=got.at[slot],
            send_sem=ss_sem.at[row], recv_sem=sr_sem.at[slot],
            device_id=device, device_id_type=MESH,
        )

    def plane_copy(which):
        part = pl.ds(which * half, half)
        return pltpu.make_async_remote_copy(
            src_ref=qbuf.at[part], dst_ref=qbuf.at[part],
            send_sem=ps_sem, recv_sem=pr_sem,
            device_id=device_of((1 - plane) * half + spot)[1], device_id_type=MESH,
        )

    def send_query(d, carry):
        p = plane * half + lax.rem(spot + d, half)
        query_copy(me, p, device_of(p)[1]).start()
        return carry

    small[3].wait()
    lax.fori_loop(1, half, send_query, 0)
    for copy in small[:3]:
        copy.wait()

    stored = lax.broadcasted_iota(I32, (slab_rows, LANES), 0) + mesh_me * slab_rows
    picked = jnp.zeros((slab_rows, LANES), I32)
    for b in range(home_ref.shape[0]):
        hit = home_ref[b : b + 1, :] == stored
        picked = jnp.where(hit, len_ref[b : b + 1, :], picked)
    ones = jnp.ones((LANES, LANES), BF16)
    lens[...] = jnp.dot(
        picked.astype(F32).astype(BF16), ones, preferred_element_type=F32
    ).astype(I32)

    count = cand_ref.shape[1]
    cand = cand_ref[...]
    low = lax.broadcasted_iota(I32, (LANES, count), 0) == lax.rem(cand, LANES)
    low = jnp.where(low, 1.0, 0.0).astype(BF16)
    home = home_ref[...]
    blocks = home.shape[0]
    high = lax.broadcasted_iota(I32, (blocks, count), 0) == cand // LANES
    for k, part in enumerate((home // slab_rows, lax.rem(home, slab_rows))):
        table = jnp.dot(part.astype(F32).astype(BF16), low, preferred_element_type=F32)
        where_row[k : k + 1, :] = jnp.sum(
            jnp.where(high, table, 0.0), axis=0, keepdims=True
        ).astype(I32)

    def wait_query(d, carry):
        p = plane * half + lax.rem(spot + d, half)
        query_copy(p, p, device_of(p)[1]).wait_recv()
        return carry

    lax.fori_loop(1, half, wait_query, 0)
    plane_copy(plane).start()

    columns = tile * tokens
    tiles = half // tile
    group = lax.broadcasted_iota(I32, (tile, columns), 0)
    member = lax.broadcasted_iota(I32, (tile, columns), 1) // tokens
    adder = jnp.where(group == member, 1.0, 0.0).astype(BF16)

    def one_tile(b, carry):
        @pl.when(b == tiles)
        def _():
            plane_copy(1 - plane).wait_recv()

        t = lax.rem(plane * tiles + b, 2 * tiles)
        query_t[...] = qbuf[pl.ds(t * tile, tile)].reshape(columns, width).T

        for r in range(0, slab_rows, band):
            live = lens[r : r + band, :]

            def some_slots(g, top):
                if r == 0:

                    @pl.when(b == 0)
                    def _():
                        load(g).wait()

                block = slab[pl.ds(g * chunk, chunk), r : r + band, :]
                similar = jnp.dot(
                    block.reshape(chunk * band, width), query_t[...],
                    preferred_element_type=F32,
                )
                for u in range(chunk):
                    inside = live > g * chunk + u
                    row = similar[u * band : (u + 1) * band]
                    top = tuple(
                        jnp.maximum(
                            old,
                            jnp.where(inside, row[:, k * LANES : (k + 1) * LANES], -1e30),
                        )
                        for k, old in enumerate(top)
                    )
                return top

            start = tuple(
                jnp.full((band, LANES), -1e30, F32) for _ in range(columns // LANES)
            )
            top = lax.fori_loop(0, chunks, some_slots, start)
            best[r : r + band, :] = jnp.concatenate(top, axis=1)
        hi, mid, lo = split3(best[...])
        scores = dot_nt(adder, lo) + dot_nt(adder, mid) + dot_nt(adder, hi)
        for i in range(tile):
            p = t * tile + i
            sent[pl.ds(p, 1)] = scores[i : i + 1].reshape(1, 1, slab_rows)

            @pl.when(p != me)
            def _():
                score_copy(p, mesh_me, device_of(p)[1]).start()

            @pl.when(p == me)
            def _():
                got[pl.ds(mesh_me, 1)] = scores[i : i + 1].reshape(1, 1, slab_rows)

        return carry

    lax.fori_loop(0, 2 * tiles, one_tile, 0)

    def wait_scores(d, carry):
        p, slot, device = peer(d)
        score_copy(p, slot, device).wait_recv()
        return carry

    lax.fori_loop(1, shards, wait_scores, 0)
    table = got[...].reshape(shards, slab_rows)
    offset = lax.broadcasted_iota(I32, (slab_rows, count), 0) == where_row[1:2, :]
    offset = jnp.where(offset, 1.0, 0.0).astype(BF16)
    hi, mid, lo = split3(table)
    dot = functools.partial(jnp.dot, preferred_element_type=F32)
    found = (dot(hi, offset) + dot(mid, offset)) + dot(lo, offset)
    shard = lax.broadcasted_iota(I32, (shards, count), 0) == where_row[0:1, :]
    score = jnp.sum(jnp.where(shard, found, 0.0), axis=0, keepdims=True)

    down = jnp.transpose(jnp.broadcast_to(score, (LANES, count)))
    mine = lax.broadcasted_iota(I32, (count, LANES), 0)
    rank = jnp.zeros((count, LANES), F32)
    for k in range(0, count, LANES):
        other = lax.broadcasted_iota(I32, (count, LANES), 1) + k
        across = score[:, k : k + LANES]
        ahead = (across > down) | ((across == down) & (other < mine))
        rank += jnp.where(ahead, 1.0, 0.0)
    rank = jnp.dot(rank.astype(BF16), ones, preferred_element_type=F32)
    slot = lax.broadcasted_iota(I32, (count, LANES), 1).astype(F32)
    ranked = jnp.sum(jnp.where(rank == slot, down, 0.0), axis=0, keepdims=True)
    out_ref[...] = ranked[:, : out_ref.shape[1]]

    def wait_sends(d, carry):
        p, slot, device = peer(d)
        score_copy(p, slot, device).wait_send()
        return carry

    lax.fori_loop(1, shards, wait_sends, 0)

    def wait_queries(d, carry):
        p = plane * half + lax.rem(spot + d, half)
        query_copy(p, p, device_of(p)[1]).wait_send()
        return carry

    lax.fori_loop(1, half, wait_queries, 0)
    plane_copy(plane).wait_send()


def on_device(queries, passages, token_lengths, candidates, passage_home):
    inner = lax.axis_size("query")
    shards = lax.axis_size("corpus") * inner
    slab_rows, slots, width = passages.shape
    tokens = queries.shape[1]
    count = candidates.shape[1]
    tile = max(1, COLUMNS // tokens)
    while (shards // 2) % tile:
        tile -= 1
    chunk = next(c for c in range(CHUNK, 0, -1) if slots % c == 0)
    band = BAND if slab_rows % BAND == 0 else slab_rows
    by_slot = jnp.transpose(passages, (1, 0, 2))
    vmem = pl.BlockSpec(memory_space=pltpu.VMEM)
    return pl.pallas_call(
        functools.partial(kernel, shards, inner, tile, chunk, band),
        out_shape=jax.ShapeDtypeStruct((1, TOPK), F32),
        in_specs=[pl.BlockSpec(memory_space=pltpu.HBM)] * 5,
        out_specs=vmem,
        scratch_shapes=[
            pltpu.VMEM((len(token_lengths) // LANES, LANES), I32),
            pltpu.VMEM(candidates.shape, I32),
            pltpu.VMEM((len(passage_home) // LANES, LANES), I32),
            pltpu.VMEM(by_slot.shape, BF16),
            pltpu.VMEM((width, tile * tokens), BF16),
            pltpu.VMEM((shards, tokens, width), BF16),
            pltpu.VMEM((slab_rows, LANES), I32),
            pltpu.VMEM((slab_rows, tile * tokens), F32),
            pltpu.VMEM((shards, 1, slab_rows), F32),
            pltpu.VMEM((shards, 1, slab_rows), F32),
            pltpu.VMEM((8, count), I32),
            pltpu.SemaphoreType.DMA((4,)),
            pltpu.SemaphoreType.DMA((slots // chunk,)),
            pltpu.SemaphoreType.DMA((shards,)),
            pltpu.SemaphoreType.DMA((shards,)),
            pltpu.SemaphoreType.DMA,
            pltpu.SemaphoreType.DMA,
            pltpu.SemaphoreType.DMA((shards,)),
            pltpu.SemaphoreType.DMA((shards,)),
        ],
        compiler_params=pltpu.CompilerParams(
            collective_id=0, has_side_effects=True, vmem_limit_bytes=56 * 1024 * 1024
        ),
    )(
        queries,
        by_slot,
        token_lengths.reshape(-1, LANES),
        candidates,
        passage_home.reshape(-1, LANES),
    )


def solution(mesh):
    placed = (
        P(("groups", "corpus", "query"), None, None),
        P(("groups", "corpus", "query"), None, None),
        P("groups"),
        P(("groups", "corpus", "query"), None),
        P("groups"),
    )
    return jax.shard_map(
        on_device,
        mesh=mesh,
        in_specs=placed,
        out_specs=P(("groups", "corpus", "query"), None),
        check_vma=False,
    )
```

```python
import functools

import jax
import jax.numpy as jnp
from jax import lax
from jax.experimental import pallas as pl
from jax.experimental.pallas import tpu as pltpu
from jax.sharding import PartitionSpec as P

TOPK = 100
LANES = 128
CHUNK, BAND, COLUMNS = 20, 128, 256
MESH = pl.DeviceIdType.MESH
F32, BF16, I32 = jnp.float32, jnp.bfloat16, jnp.int32


def split3(x):
    hi = x.astype(BF16)
    rest = x - hi.astype(F32)
    mid = rest.astype(BF16)
    return hi, mid, (rest - mid.astype(F32)).astype(BF16)


def dot_nt(a, b):
    return lax.dot_general(a, b, (((1,), (1,)), ((), ())), preferred_element_type=F32)


def kernel(
    shards, inner, tile, chunk, band,
    q_ref, pass_ref, len_hbm, cand_hbm, home_hbm, out_ref,
    len_ref, cand_ref, home_ref, slab, query_t, qbuf, lens, best, sent, got, where_row,
    small_sem, load_sem, qs_sem, qr_sem, ps_sem, pr_sem, ss_sem, sr_sem,
):
    slots, slab_rows, width = slab.shape
    tokens = qbuf.shape[1]
    mesh_me = lax.axis_index("corpus") * inner + lax.axis_index("query")
    half = shards // 2
    plane = lax.rem(lax.axis_index("corpus"), 2)
    spot = (lax.axis_index("corpus") // 2) * inner + lax.axis_index("query")
    me = plane * half + spot

    def device_of(p):
        rest = lax.rem(p, half)
        corpus = (rest // inner) * 2 + p // half
        query = lax.rem(rest, inner)
        return corpus * inner + query, {"corpus": corpus, "query": query}

    chunks = slots // chunk

    def load(c):
        part = pl.ds(c * chunk, chunk)
        return pltpu.make_async_copy(pass_ref.at[part], slab.at[part], load_sem.at[c])

    def peer(d):
        p = lax.rem(me + d, shards)
        return p, *device_of(p)

    barrier = pltpu.get_barrier_semaphore()

    def greet(d, carry):
        pl.semaphore_signal(barrier, inc=1, device_id=peer(d)[2], device_id_type=MESH)
        return carry

    lax.fori_loop(1, shards, greet, 0, unroll=True)
    small = [
        pltpu.make_async_copy(src, dst, small_sem.at[k])
        for k, (src, dst) in enumerate(
            (
                (home_hbm, home_ref),
                (len_hbm, len_ref),
                (cand_hbm, cand_ref),
                (q_ref, qbuf.at[pl.ds(me, 1)]),
            )
        )
    ]
    for copy in small:
        copy.start()
    for c in range(chunks):
        load(c).start()
    small[0].wait()
    small[1].wait()

    stored = lax.broadcasted_iota(I32, (slab_rows, LANES), 0) + mesh_me * slab_rows
    picked = jnp.zeros((slab_rows, LANES), I32)
    for b in range(home_ref.shape[0]):
        hit = home_ref[b : b + 1, :] == stored
        picked = jnp.where(hit, len_ref[b : b + 1, :], picked)
    ones = jnp.ones((LANES, LANES), BF16)
    lens[...] = jnp.dot(
        picked.astype(F32).astype(BF16), ones, preferred_element_type=F32
    ).astype(I32)
    small[2].wait()
    small[3].wait()
    pl.semaphore_wait(barrier, shards - 1)

    def query_copy(slot, sem_s, device):
        return pltpu.make_async_remote_copy(
            src_ref=qbuf.at[pl.ds(me, 1)], dst_ref=qbuf.at[pl.ds(slot, 1)],
            send_sem=qs_sem.at[sem_s], recv_sem=qr_sem.at[slot],
            device_id=device, device_id_type=MESH,
        )

    def score_copy(row, slot, device):
        return pltpu.make_async_remote_copy(
            src_ref=sent.at[row], dst_ref=got.at[slot],
            send_sem=ss_sem.at[row], recv_sem=sr_sem.at[slot],
            device_id=device, device_id_type=MESH,
        )

    def plane_copy(which):
        part = pl.ds(which * half, half)
        return pltpu.make_async_remote_copy(
            src_ref=qbuf.at[part], dst_ref=qbuf.at[part],
            send_sem=ps_sem, recv_sem=pr_sem,
            device_id=device_of((1 - plane) * half + spot)[1], device_id_type=MESH,
        )

    def send_query(d, carry):
        p = plane * half + lax.rem(spot + d, half)
        query_copy(me, p, device_of(p)[1]).start()
        return carry

    lax.fori_loop(1, half, send_query, 0, unroll=True)

    count = cand_ref.shape[1]
    cand = cand_ref[...]
    low = lax.broadcasted_iota(I32, (LANES, count), 0) == lax.rem(cand, LANES)
    low = jnp.where(low, 1.0, 0.0).astype(BF16)
    home = home_ref[...]
    blocks = home.shape[0]
    high = lax.broadcasted_iota(I32, (blocks, count), 0) == cand // LANES
    for k, part in enumerate((home // slab_rows, lax.rem(home, slab_rows))):
        table = jnp.dot(part.astype(F32).astype(BF16), low, preferred_element_type=F32)
        where_row[k : k + 1, :] = jnp.sum(
            jnp.where(high, table, 0.0), axis=0, keepdims=True
        ).astype(I32)

    def wait_query(d, carry):
        p = plane * half + lax.rem(spot + d, half)
        query_copy(p, p, device_of(p)[1]).wait_recv()
        return carry

    lax.fori_loop(1, half, wait_query, 0, unroll=True)
    plane_copy(plane).start()

    columns = tile * tokens
    tiles = half // tile
    group = lax.broadcasted_iota(I32, (tile, columns), 0)
    member = lax.broadcasted_iota(I32, (tile, columns), 1) // tokens
    adder = jnp.where(group == member, 1.0, 0.0).astype(BF16)

    def one_tile(b, carry):
        @pl.when(b == tiles)
        def _():
            plane_copy(1 - plane).wait_recv()

        t = lax.rem(plane * tiles + b, 2 * tiles)
        query_t[...] = qbuf[pl.ds(t * tile, tile)].reshape(columns, width).T

        for r in range(0, slab_rows, band):
            live = lens[r : r + band, :]

            def some_slots(g, top):
                if r == 0:

                    @pl.when(b == 0)
                    def _():
                        load(g).wait()

                block = slab[pl.ds(g * chunk, chunk), r : r + band, :]
                similar = jnp.dot(
                    block.reshape(chunk * band, width), query_t[...],
                    preferred_element_type=F32,
                )
                for u in range(chunk):
                    inside = live > g * chunk + u
                    row = similar[u * band : (u + 1) * band]
                    top = tuple(
                        jnp.maximum(
                            old,
                            jnp.where(inside, row[:, k * LANES : (k + 1) * LANES], -1e30),
                        )
                        for k, old in enumerate(top)
                    )
                return top

            start = tuple(
                jnp.full((band, LANES), -1e30, F32) for _ in range(columns // LANES)
            )
            top = lax.fori_loop(0, chunks, some_slots, start)
            best[r : r + band, :] = jnp.concatenate(top, axis=1)
        hi, mid, lo = split3(best[...])
        scores = dot_nt(adder, lo) + dot_nt(adder, mid) + dot_nt(adder, hi)
        for i in range(tile):
            p = t * tile + i
            sent[pl.ds(p, 1)] = scores[i : i + 1].reshape(1, 1, slab_rows)

            @pl.when(p != me)
            def _():
                score_copy(p, mesh_me, device_of(p)[1]).start()

            @pl.when(p == me)
            def _():
                got[pl.ds(mesh_me, 1)] = scores[i : i + 1].reshape(1, 1, slab_rows)

        return carry

    lax.fori_loop(0, 2 * tiles, one_tile, 0)

    def wait_scores(d, carry):
        p, slot, device = peer(d)
        score_copy(p, slot, device).wait_recv()
        return carry

    lax.fori_loop(1, shards, wait_scores, 0, unroll=True)
    table = got[...].reshape(shards, slab_rows)
    offset = lax.broadcasted_iota(I32, (slab_rows, count), 0) == where_row[1:2, :]
    offset = jnp.where(offset, 1.0, 0.0).astype(BF16)
    hi, mid, lo = split3(table)
    dot = functools.partial(jnp.dot, preferred_element_type=F32)
    found = (dot(hi, offset) + dot(mid, offset)) + dot(lo, offset)
    shard = lax.broadcasted_iota(I32, (shards, count), 0) == where_row[0:1, :]
    score = jnp.sum(jnp.where(shard, found, 0.0), axis=0, keepdims=True)

    down = jnp.transpose(jnp.broadcast_to(score, (LANES, count)))
    mine = lax.broadcasted_iota(I32, (count, LANES), 0)
    rank = jnp.zeros((count, LANES), F32)
    for k in range(0, count, LANES):
        other = lax.broadcasted_iota(I32, (count, LANES), 1) + k
        across = score[:, k : k + LANES]
        ahead = (across > down) | ((across == down) & (other < mine))
        rank += jnp.where(ahead, 1.0, 0.0)
    rank = jnp.dot(rank.astype(BF16), ones, preferred_element_type=F32)
    slot = lax.broadcasted_iota(I32, (count, LANES), 1).astype(F32)
    ranked = jnp.sum(jnp.where(rank == slot, down, 0.0), axis=0, keepdims=True)
    out_ref[...] = ranked[:, : out_ref.shape[1]]

    def wait_sends(d, carry):
        p, slot, device = peer(d)
        score_copy(p, slot, device).wait_send()
        return carry

    lax.fori_loop(1, shards, wait_sends, 0, unroll=True)

    def wait_queries(d, carry):
        p = plane * half + lax.rem(spot + d, half)
        query_copy(p, p, device_of(p)[1]).wait_send()
        return carry

    lax.fori_loop(1, half, wait_queries, 0, unroll=True)
    plane_copy(plane).wait_send()


def on_device(queries, passages, token_lengths, candidates, passage_home):
    inner = lax.axis_size("query")
    shards = lax.axis_size("corpus") * inner
    slab_rows, slots, width = passages.shape
    tokens = queries.shape[1]
    count = candidates.shape[1]
    tile = max(1, COLUMNS // tokens)
    while (shards // 2) % tile:
        tile -= 1
    chunk = next(c for c in range(CHUNK, 0, -1) if slots % c == 0)
    band = BAND if slab_rows % BAND == 0 else slab_rows
    by_slot = jnp.transpose(passages, (1, 0, 2))
    vmem = pl.BlockSpec(memory_space=pltpu.VMEM)
    return pl.pallas_call(
        functools.partial(kernel, shards, inner, tile, chunk, band),
        out_shape=jax.ShapeDtypeStruct((1, TOPK), F32),
        in_specs=[pl.BlockSpec(memory_space=pltpu.HBM)] * 5,
        out_specs=vmem,
        scratch_shapes=[
            pltpu.VMEM((len(token_lengths) // LANES, LANES), I32),
            pltpu.VMEM(candidates.shape, I32),
            pltpu.VMEM((len(passage_home) // LANES, LANES), I32),
            pltpu.VMEM(by_slot.shape, BF16),
            pltpu.VMEM((width, tile * tokens), BF16),
            pltpu.VMEM((shards, tokens, width), BF16),
            pltpu.VMEM((slab_rows, LANES), I32),
            pltpu.VMEM((slab_rows, tile * tokens), F32),
            pltpu.VMEM((shards, 1, slab_rows), F32),
            pltpu.VMEM((shards, 1, slab_rows), F32),
            pltpu.VMEM((8, count), I32),
            pltpu.SemaphoreType.DMA((4,)),
            pltpu.SemaphoreType.DMA((slots // chunk,)),
            pltpu.SemaphoreType.DMA((shards,)),
            pltpu.SemaphoreType.DMA((shards,)),
            pltpu.SemaphoreType.DMA,
            pltpu.SemaphoreType.DMA,
            pltpu.SemaphoreType.DMA((shards,)),
            pltpu.SemaphoreType.DMA((shards,)),
        ],
        compiler_params=pltpu.CompilerParams(
            collective_id=0, has_side_effects=True, vmem_limit_bytes=56 * 1024 * 1024
        ),
    )(
        queries,
        by_slot,
        token_lengths.reshape(-1, LANES),
        candidates,
        passage_home.reshape(-1, LANES),
    )


def solution(mesh):
    placed = (
        P(("groups", "corpus", "query"), None, None),
        P(("groups", "corpus", "query"), None, None),
        P("groups"),
        P(("groups", "corpus", "query"), None),
        P("groups"),
    )
    return jax.shard_map(
        on_device,
        mesh=mesh,
        in_specs=placed,
        out_specs=P(("groups", "corpus", "query"), None),
        check_vma=False,
    )
```
